128 devices in a mesh: dp: 16 (over x_hi, y, core), cores: 8 (over z, x_lo).
Axes of the slice: x: 4 (x_hi: 2, x_lo: 2; x = x_hi * 2 + x_lo), y: 4, z: 4, core: 2. Of those that a mesh axis runs over, the one named last changes fastest.
Arguments:
- data: bfloat16 [65536, 768], P('dp'), may hold values from -6 to 6
- data_pot: bfloat16 [65536], P('dp'), may hold values from -6 to 6
- coreset: bfloat16 [4096, 768], P('cores')
- core_pot: bfloat16 [4096], P('cores'), may hold values from -12 to 12
Outputs:
- core_grad: float32 [4096, 768], P('cores', 'dp')
The draws below stay inside these ranges and needn't reach their ends.
All inputs are finite; a program needn't handle non-finite values.
Results may differ from the reference program's by a relative error of at most 0.0095.
Values may be sent and summed in bfloat16 or wider, within the bound.
No kernel may reach another device: no remote copies, remote signals or barrier semaphores. Data moves between devices by JAX's collectives and lax.ppermute only.
A program may use at most 128 MiB of HBM per device.

```python
import math
import jax
import jax.numpy as jnp
from jax import lax

D = 768
N_ROWS = 65536
M = 4096


def draw_coreset(key, part):
    key = jax.random.fold_in(key, 7)
    values = jnp.clip(jax.random.normal(key, (M, D), jnp.float32), -6.0, 6.0) * 0.1
    return values.astype(jnp.bfloat16)


def levels(key, shape, cuts, smallest, largest):
    factor_of, own = 1.0, jax.random.fold_in(key, 6)
    for dim, shards_of in cuts:
        steps = jnp.exp(jax.random.uniform(jax.random.fold_in(own, dim), (shards_of,), jnp.float32, smallest / len(cuts), largest / len(cuts)))
        factor_of = factor_of * jnp.repeat(steps, shape[dim] // shards_of).reshape([-1 if axis == dim else 1 for axis in range(len(shape))])
    return factor_of


def bell_draw(stream_key, dims, scale, bound, shards=(), held_as=jnp.bfloat16):
    entries = scale * jax.random.normal(stream_key, dims, jnp.float32)
    if shards:
        entries = entries * levels(stream_key, dims, shards, -0.22, 0.18)
    return jnp.clip(entries, -bound, bound).astype(held_as)


def setup_inputs(seed: int = 0) -> dict:
    seeds = jax.random.split(jax.random.key(seed), 5)
    return {
        "data": bell_draw(seeds[0], (N_ROWS, D), 1.0, 6.0, ((0, 16),)),
        "data_pot": bell_draw(seeds[1], (N_ROWS,), 1.0, 6.0, ((0, 16),)),
        "coreset": draw_coreset(jax.random.fold_in(seeds[4], 71), 0),
        "core_pot": bell_draw(seeds[3], (M,), 2.0, 12.0, ((0, 8),)),
    }


def barycenter(queries, keys, potential, scale):
    scores = potential.astype(jnp.float32)[None, :] + scale * lax.dot_general(queries, keys, (((1,), (1,)), ((), ())), preferred_element_type=jnp.float32)
    top = lax.optimization_barrier(jnp.max(scores, axis=1, keepdims=True))
    weights = jnp.exp(scores - top).astype(jnp.bfloat16)
    total = lax.optimization_barrier(jnp.sum(weights.astype(jnp.float32), axis=1))
    summed = jnp.dot(weights, keys, preferred_element_type=jnp.float32)
    return summed / total[:, None]

def reference(data, data_pot, coreset, core_pot):
    scale = 30.0 / math.sqrt(D)
    block = math.gcd(M, 256)
    blocks = coreset.reshape(M // block, block, D)

    def one_block(queries):
        return barycenter(queries, coreset, core_pot, scale) - barycenter(queries, data, data_pot, scale)
    result = lax.map(one_block, blocks)
    return result.reshape(M, D)
```

```python
import functools
import math

import jax
import jax.numpy as jnp
from jax import lax
from jax.experimental import pallas as pl
from jax.experimental.pallas import tpu as pltpu
from jax.sharding import PartitionSpec as P

ROWS = 48
STATS = 8
TAIL = 16
VMEM_LIMIT = 48 * 2**20


def whole():
    return pl.BlockSpec(memory_space=pltpu.VMEM)


def fold(op, value):
    out = value[:, :128]
    for k in range(128, value.shape[1], 128):
        out = op(out, value[:, k : k + 128])
    return out


def write_halves(core, acc, top, total, send_ref, keep_ref, stat_ref):
    count, width = acc.shape
    lane = lax.broadcasted_iota(jnp.int32, (count, 128), 1)
    stats = jnp.where(lane == 0, top, total).T[:STATS]
    stat_ref[...] = stats
    half = width // 2
    send_ref[half:, :] = stats
    for j in range(0, width, 8 * ROWS):
        turned = acc[:, j : j + 8 * ROWS].T
        for i in range(4):
            first = turned[2 * ROWS * i : 2 * ROWS * i + ROWS]
            second = turned[2 * ROWS * i + ROWS : 2 * ROWS * (i + 1)]
            at = j // 2 + ROWS * i
            keep_ref[at : at + ROWS, :] = jnp.where(core == 0, first, second)
            send_ref[at : at + ROWS, :] = jnp.where(core == 0, second, first)


def cross_kernel(
    core_ref, pot_ref, query_ref, data_ref, send_ref, keep_ref, stat_ref,
    held, scores, weights, acc, top, total, sems,
):
    count, width = data_ref.shape
    cuts = (0, 512, 1024, count)
    step = 512
    part = width // 2
    scale = 30.0 / math.sqrt(width)
    copies = {
        a: pltpu.make_async_copy(data_ref.at[pl.ds(a, b - a)], held.at[pl.ds(a, b - a)], sems.at[i])
        for i, (a, b) in enumerate(zip(cuts, cuts[1:]))
    }
    for copy in copies.values():
        copy.start()
    for i in range(0, count, step):
        if i in copies:
            copies[i].wait()
        s = lax.dot_general(
            query_ref[...], held[i : i + step, :], (((1,), (1,)), ((), ())), preferred_element_type=jnp.float32
        )
        s = s * scale + pot_ref[:, i : i + step].astype(jnp.float32)
        scores[:, i : i + step] = s
        largest = fold(jnp.maximum, s)
        top[...] = largest if i == 0 else jnp.maximum(top[...], largest)
    top[...] = jnp.broadcast_to(jnp.max(top[...], axis=1, keepdims=True), top.shape)

    def soften(i, first, last):
        added = None
        for k in range(first, last, 128):
            p = jnp.exp(scores[:, i + k : i + k + 128] - top[...])
            weights[(i // step) % 2, :, k : k + 128] = p.astype(jnp.bfloat16)
            added = p if added is None else added + p
        total[...] = added if i + first == 0 else total[...] + added

    soften(0, 0, step)
    for i in range(0, count, step):
        for t in range(2):
            if i + step < count:
                soften(i + step, step // 2 * t, step // 2 * (t + 1))
            columns = slice(part * t, part * (t + 1))
            d = jnp.dot(weights[(i // step) % 2], held[i : i + step, columns], preferred_element_type=jnp.float32)
            acc[:, columns] = d if i == 0 else acc[:, columns] + d
    summed = jnp.sum(total[...], axis=1, keepdims=True)
    write_halves(core_ref[0], acc, top[...], summed, send_ref, keep_ref, stat_ref)


def self_kernel(core_ref, query_ref, key_ref, send_ref, keep_ref, stat_ref, acc):
    count, width = query_ref.shape
    number = key_ref.shape[0] - TAIL
    scale = 30.0 / math.sqrt(width)
    keys = key_ref[:number, :]
    pot = key_ref[number:, :number].astype(jnp.float32)[:1]
    s = scale * lax.dot_general(query_ref[...], keys, (((1,), (1,)), ((), ())), preferred_element_type=jnp.float32)
    s = s + pot
    top = jnp.max(s, axis=1, keepdims=True)
    p = jnp.exp(s - top)
    total = jnp.sum(p, axis=1, keepdims=True)
    acc[...] = jnp.dot(p.astype(jnp.bfloat16), keys, preferred_element_type=jnp.float32)
    top = jnp.broadcast_to(top, (count, 128))
    write_halves(core_ref[0], acc, top, total, send_ref, keep_ref, stat_ref)


def pair_kernel(keep_u, stat_u, come_u, keep_v, stat_v, come_v, out_ref):
    half = keep_u.shape[0]
    kept = []
    for n, (keep, stat, come) in enumerate(((keep_u, stat_u, come_u), (keep_v, stat_v, come_v))):
        other = come[half:, :]
        top = jnp.maximum(stat[0:1], other[0:1])
        left, right = jnp.exp(stat[0:1] - top), jnp.exp(other[0:1] - top)
        kept += [top, stat[1:2] * left + other[1:2] * right]
        for i in range(half // ROWS):
            rows = slice(ROWS * i, ROWS * (i + 1))
            out_ref[i, ROWS * n : ROWS * (n + 1), :] = (keep[rows] * left + come[rows] * right).astype(jnp.bfloat16)
    exact = jnp.concatenate(kept, 0)
    high = exact.astype(jnp.bfloat16).astype(jnp.float32)
    middle = (exact - high).astype(jnp.bfloat16).astype(jnp.float32)
    low = exact - high - middle
    tail = jnp.concatenate([high, middle, low, jnp.zeros_like(low)], 0).astype(jnp.bfloat16)
    for i in range(half // ROWS):
        out_ref[i, 2 * ROWS :, :] = tail


def last_kernel(come_ref, out_ref):
    chips = come_ref.shape[0]
    stats = []
    for i in range(chips):
        tail = come_ref[i, 2 * ROWS :, :].astype(jnp.float32)
        stats.append(tail[0:4] + tail[4:8] + tail[8:12])
    results = []
    for n in range(2):
        tops = [s[2 * n : 2 * n + 1] for s in stats]
        top = functools.reduce(jnp.maximum, tops)
        shares = [jnp.exp(t - top) for t in tops]
        total = sum(share * s[2 * n + 1 : 2 * n + 2] for share, s in zip(shares, stats))
        summed = sum(
            share * come_ref[i, ROWS * n : ROWS * (n + 1), :].astype(jnp.float32) for i, share in enumerate(shares)
        )
        results.append(summed / total)
    out_ref[...] = results[1] - results[0]


def on_device(data, data_pot, coreset, core_pot):
    count, width = coreset.shape
    half = width // 2
    chips = width // (2 * ROWS)
    position = lax.axis_index("dp")
    shards, blocks = lax.axis_size("dp"), lax.axis_size("cores")
    core = (position % 2).astype(jnp.int32).reshape(1)
    f32 = jnp.float32
    params = pltpu.CompilerParams(vmem_limit_bytes=VMEM_LIMIT)

    number = count * blocks // shards
    own = lax.dynamic_slice_in_dim(coreset, (position % 2) * number, number, 0)
    own_pot = lax.dynamic_slice_in_dim(core_pot, (position % 2) * number, number, 0)
    row = jnp.pad(own_pot[None, :], ((0, TAIL - 1), (0, width - number)))
    pairs = [(d * blocks + (c + d // 2) % blocks, d * blocks + c) for d in range(shards) for c in range(blocks)]
    keys = lax.ppermute(jnp.concatenate([own, row], 0), ("dp", "cores"), pairs)

    outs = [
        jax.ShapeDtypeStruct((half + STATS, count), f32),
        jax.ShapeDtypeStruct((half, count), f32),
        jax.ShapeDtypeStruct((STATS, count), f32),
    ]
    smem = pl.BlockSpec(memory_space=pltpu.SMEM)
    items = data.shape[0]
    send_u, keep_u, stat_u = pl.pallas_call(
        cross_kernel,
        out_shape=outs,
        in_specs=[smem, whole(), whole(), pl.BlockSpec(memory_space=pl.ANY)],
        out_specs=[whole()] * 3,
        scratch_shapes=[
            pltpu.VMEM((items, width), jnp.bfloat16),
            pltpu.VMEM((count, items), f32),
            pltpu.VMEM((2, count, 512), jnp.bfloat16),
            pltpu.VMEM((count, width), f32),
            pltpu.VMEM((count, 128), f32),
            pltpu.VMEM((count, 128), f32),
            pltpu.SemaphoreType.DMA((3,)),
        ],
        compiler_params=params,
        cost_estimate=pl.CostEstimate(
            flops=4 * count * items * width, bytes_accessed=2 * items * width, transcendentals=count * items
        ),
        name="cross",
    )(core, data_pot.reshape(1, items), coreset, data)
    swap = [(d, d ^ 1) for d in range(shards)]
    come_u = lax.ppermute(send_u, "dp", swap)
    send_v, keep_v, stat_v = pl.pallas_call(
        self_kernel,
        out_shape=outs,
        in_specs=[smem, whole(), whole()],
        out_specs=[whole()] * 3,
        scratch_shapes=[pltpu.VMEM((count, width), f32)],
        compiler_params=params,
        cost_estimate=pl.CostEstimate(
            flops=4 * count * number * width, bytes_accessed=4 * count * width, transcendentals=count * number
        ),
        name="self",
    )(core, coreset, keys)
    come_v = lax.ppermute(send_v, "dp", swap)
    merged = pl.pallas_call(
        pair_kernel,
        out_shape=jax.ShapeDtypeStruct((chips, 2 * ROWS + TAIL, count), jnp.bfloat16),
        in_specs=[whole()] * 6,
        out_specs=whole(),
        compiler_params=params,
        name="pair",
    )(keep_u, stat_u, come_u, keep_v, stat_v, come_v)
    groups = [[2 * i + k for i in range(chips)] for k in range(2)]
    come = lax.all_to_all(merged, "dp", 0, 0, axis_index_groups=groups, tiled=True)
    return pl.pallas_call(
        last_kernel,
        out_shape=jax.ShapeDtypeStruct((ROWS, count), f32),
        in_specs=[whole()],
        out_specs=whole(),
        compiler_params=params,
        name="last",
    )(come).T


def solution(mesh):
    return jax.shard_map(
        on_device,
        mesh=mesh,
        in_specs=(P("dp", None), P("dp"), P("cores", None), P("cores")),
        out_specs=P("cores", "dp"),
        check_vma=False,
    )
```

```python
import functools
import math

import jax
import jax.numpy as jnp
from jax import lax
from jax.experimental import pallas as pl
from jax.experimental.pallas import tpu as pltpu
from jax.sharding import PartitionSpec as P

ROWS = 48
STATS = 8
TAIL = 16
REST = 8
WHENCE = (((0, 0), (2, 1)), ((0, 1), (2, 0)), ((1, 0), (3, 1)), ((1, 1), (3, 0)))
VMEM_LIMIT = 16 * 2**20


def whole():
    return pl.BlockSpec(memory_space=pltpu.VMEM)


def fold(op, value):
    out = value[:, :128]
    for k in range(128, value.shape[1], 128):
        out = op(out, value[:, k : k + 128])
    return out


def write_halves(core, acc, top, total, send_ref, keep_ref, stat_ref):
    count, width = acc.shape
    lane = lax.broadcasted_iota(jnp.int32, (count, 128), 1)
    stats = jnp.where(lane == 0, top, total).T[:STATS]
    stat_ref[...] = stats
    half = width // 2
    send_ref[half:, :] = stats
    for j in range(0, width, 8 * ROWS):
        turned = acc[:, j : j + 8 * ROWS].T
        for i in range(4):
            first = turned[2 * ROWS * i : 2 * ROWS * i + ROWS]
            second = turned[2 * ROWS * i + ROWS : 2 * ROWS * (i + 1)]
            at = j // 2 + ROWS * i
            keep_ref[at : at + ROWS, :] = jnp.where(core == 0, first, second)
            send_ref[at : at + ROWS, :] = jnp.where(core == 0, second, first)


def begin_kernel(core_ref, half_ref, out_ref):
    out_ref[...] = jnp.full(out_ref.shape, core_ref[0] + half_ref[0], out_ref.dtype)


def pack_kernel(after_ref, pot_ref, points_ref, key_ref):
    del after_ref
    number, width = points_ref.shape
    key_ref[:number, :] = points_ref[...]
    pot = pot_ref[...].astype(jnp.float32).reshape(1, number)
    row = jnp.concatenate([pot, jnp.zeros((1, width - number), jnp.float32)], 1)
    key_ref[number:, :] = jnp.broadcast_to(row, (TAIL, width)).astype(jnp.bfloat16)


def weigh_kernel(pot_ref, query_ref, data_ref, weights_ref, top_ref, total_ref, scores):
    count, width = data_ref.shape
    step = 512
    scale = 30.0 / math.sqrt(width)
    query = query_ref[: scores.shape[0], :]
    for i in range(0, count, step):
        s = lax.dot_general(
            query, data_ref[i : i + step, :], (((1,), (1,)), ((), ())), preferred_element_type=jnp.float32
        )
        s = s * scale + pot_ref[i : i + step].astype(jnp.float32).reshape(1, step)
        scores[:, i : i + step] = s
        largest = fold(jnp.maximum, s)
        top_ref[...] = largest if i == 0 else jnp.maximum(top_ref[...], largest)
    top_ref[...] = jnp.broadcast_to(jnp.max(top_ref[...], axis=1, keepdims=True), top_ref.shape)
    for i in range(0, count, step):
        added = None
        for k in range(i, i + step, 128):
            p = jnp.exp(scores[:, k : k + 128] - top_ref[...])
            weights_ref[:, k : k + 128] = p.astype(jnp.bfloat16)
            added = p if added is None else added + p
        total_ref[...] = added if i == 0 else total_ref[...] + added


def sum_kernel(core_ref, weights_ref, data_ref, top_ref, total_ref, send_ref, keep_ref, stat_ref, acc):
    acc[...] = jnp.dot(weights_ref[...], data_ref[...], preferred_element_type=jnp.float32)
    summed = jnp.sum(total_ref[...], axis=1, keepdims=True)
    write_halves(core_ref[0], acc, top_ref[...], summed, send_ref, keep_ref, stat_ref)


def self_kernel(core_ref, half_ref, query_ref, key_ref, after_ref, send_ref, keep_ref, stat_ref, acc):
    del after_ref
    count, width = acc.shape
    number = key_ref.shape[0] - TAIL
    scale = 30.0 / math.sqrt(width)
    query = query_ref[pl.ds(pl.multiple_of(half_ref[0] * count, count), count), :]
    keys = key_ref[:number, :]
    pot = key_ref[number:, :number].astype(jnp.float32)[:1]
    s = scale * lax.dot_general(query, keys, (((1,), (1,)), ((), ())), preferred_element_type=jnp.float32)
    s = s + pot
    top = jnp.max(s, axis=1, keepdims=True)
    p = jnp.exp(s - top)
    total = jnp.sum(p, axis=1, keepdims=True)
    acc[...] = jnp.dot(p.astype(jnp.bfloat16), keys, preferred_element_type=jnp.float32)
    top = jnp.broadcast_to(top, (count, 128))
    write_halves(core_ref[0], acc, top, total, send_ref, keep_ref, stat_ref)


def parted(value, number):
    pieces = []
    for _ in range(number):
        piece = value.astype(jnp.bfloat16).astype(jnp.float32)
        pieces.append(piece)
        value = value - piece
    return pieces


def pair_kernel(keep_u, stat_u, come_u, keep_v, stat_v, come_v, out_ref):
    half = keep_u.shape[0]
    merged = []
    for keep, stat, come in ((keep_u, stat_u, come_u), (keep_v, stat_v, come_v)):
        other = come[half:, :]
        top = jnp.maximum(stat[0:1], other[0:1])
        left, right = jnp.exp(stat[0:1] - top), jnp.exp(other[0:1] - top)
        merged.append((top, stat[1:2] * left + other[1:2] * right, left, right))
    (top_u, total_u, left_u, right_u), (top_v, total_v, left_v, right_v) = merged
    high, middle, low = parted(top_v, 3)
    main, rest = parted(total_v, 2)
    tail = parted(top_u, 3) + parted(total_u, 2)
    for pieces in ((high, middle), (low, main), (rest, jnp.zeros_like(rest))):
        tail.append(jnp.concatenate(pieces, 1))
    tail = jnp.concatenate(tail, 0)
    for i in range(half // ROWS):
        rows = slice(ROWS * i, ROWS * (i + 1))
        out_ref[i, :ROWS, :] = (keep_u[rows] * left_u + come_u[rows] * right_u).astype(jnp.bfloat16)
        v = keep_v[rows] * left_v + come_v[rows] * right_v
        v = jnp.concatenate([v[: ROWS // 2], v[ROWS // 2 :]], 1)
        out_ref[i, ROWS:, :] = jnp.concatenate([v, tail], 0).astype(jnp.bfloat16)


def joined(parts):
    top = functools.reduce(jnp.maximum, [t for t, _, _ in parts])
    shares = [jnp.exp(t - top) for t, _, _ in parts]
    total = sum(share * t for share, (_, t, _) in zip(shares, parts))
    return sum(share * value for share, (_, _, value) in zip(shares, parts)) / total


def last_kernel(come_ref, out_ref):
    chips = come_ref.shape[0]
    count = out_ref.shape[1] // 2
    cross, own = [], []
    for i in range(chips):
        u = come_ref[i, :ROWS, :].astype(jnp.float32)
        rest = come_ref[i, ROWS:, :].astype(jnp.float32)
        s = rest[ROWS // 2 :]
        cross.append((s[0:1] + s[1:2] + s[2:3], s[3:4] + s[4:5], u))
        top = s[5:6, :count] + s[5:6, count:] + s[6:7, :count]
        total = s[6:7, count:] + s[7:8, :count]
        own.append((jnp.concatenate([top, top], 1), jnp.concatenate([total, total], 1), rest[: ROWS // 2]))
    pull = joined(cross)
    for h in range(2):
        push = joined(own[h * chips // 2 : (h + 1) * chips // 2])
        lanes = slice(h * count, (h + 1) * count)
        out_ref[: ROWS // 2, lanes] = push[:, :count] - pull[: ROWS // 2, lanes]
        out_ref[ROWS // 2 :, lanes] = push[:, count:] - pull[ROWS // 2 :, lanes]


def on_device(data, data_pot, coreset, core_pot):
    count, width = coreset.shape
    items = data.shape[0]
    half = width // 2
    chips = width // (2 * ROWS)
    position = lax.axis_index("dp")
    shards, blocks = lax.axis_size("dp"), lax.axis_size("cores")
    core = (position % 2).astype(jnp.int32).reshape(1)
    x_hi = (position // chips).astype(jnp.int32).reshape(1)
    f32 = jnp.float32
    params = pltpu.CompilerParams(vmem_limit_bytes=VMEM_LIMIT)
    smem, anywhere = pl.BlockSpec(memory_space=pltpu.SMEM), pl.BlockSpec(memory_space=pl.ANY)

    begun = pl.pallas_call(
        begin_kernel,
        out_shape=jax.ShapeDtypeStruct((8, 128), jnp.int32),
        in_specs=[smem, smem],
        out_specs=whole(),
        compiler_params=params,
        cost_estimate=pl.CostEstimate(flops=10**11, bytes_accessed=4 * items * width, transcendentals=0),
        name="begin",
    )(core, x_hi)
    packed = pl.pallas_call(
        pack_kernel,
        out_shape=jax.ShapeDtypeStruct((count + TAIL, width), coreset.dtype),
        in_specs=[anywhere, whole(), whole()],
        out_specs=whole(),
        compiler_params=params,
        name="pack",
    )(begun, core_pot, coreset)
    pairs = []
    for d in range(shards):
        along, across = WHENCE[d // 2 % 4][d % 2]
        for c in range(blocks):
            source = (c // 2 + along) % 4 * 2 + (c % 2 ^ across)
            pairs.append((d * blocks + source, d * blocks + c))
    keys = lax.ppermute(packed, ("dp", "cores"), pairs)

    weights, top, total = pl.pallas_call(
        weigh_kernel,
        out_shape=[
            jax.ShapeDtypeStruct((count, items), jnp.bfloat16),
            jax.ShapeDtypeStruct((count, 128), f32),
            jax.ShapeDtypeStruct((count, 128), f32),
        ],
        in_specs=[whole()] * 3,
        out_specs=[whole()] * 3,
        scratch_shapes=[pltpu.VMEM((count, items), f32)],
        compiler_params=params,
        cost_estimate=pl.CostEstimate(
            flops=2 * count * items * width, bytes_accessed=2 * items * width, transcendentals=count * items
        ),
        name="weigh",
    )(data_pot, packed, data)

    def halves(number):
        return [
            jax.ShapeDtypeStruct((half + STATS, number), f32),
            jax.ShapeDtypeStruct((half, number), f32),
            jax.ShapeDtypeStruct((STATS, number), f32),
        ]

    swap = [(d, d ^ 1) for d in range(shards)]
    send_u, keep_u, stat_u = pl.pallas_call(
        sum_kernel,
        out_shape=halves(count),
        in_specs=[smem] + [whole()] * 4,
        out_specs=[whole()] * 3,
        scratch_shapes=[pltpu.VMEM((count, width), f32)],
        compiler_params=params,
        cost_estimate=pl.CostEstimate(
            flops=2 * count * items * width, bytes_accessed=2 * items * width, transcendentals=0
        ),
        name="sums",
    )(core, weights, data, top, total)
    come_u = lax.ppermute(send_u, "dp", swap)
    send_v, keep_v, stat_v = pl.pallas_call(
        self_kernel,
        out_shape=halves(count // 2),
        in_specs=[smem, smem, whole(), whole(), anywhere],
        out_specs=[whole()] * 3,
        scratch_shapes=[pltpu.VMEM((count // 2, width), f32)],
        compiler_params=params,
        cost_estimate=pl.CostEstimate(
            flops=2 * count * count * width, bytes_accessed=4 * count * width, transcendentals=count * count // 2
        ),
        name="self",
    )(core, x_hi, packed, keys, stat_u)
    come_v = lax.ppermute(send_v, "dp", swap)
    merged = pl.pallas_call(
        pair_kernel,
        out_shape=jax.ShapeDtypeStruct((chips, 3 * ROWS // 2 + REST, count), jnp.bfloat16),
        in_specs=[whole()] * 6,
        out_specs=whole(),
        compiler_params=params,
        name="pair",
    )(keep_u, stat_u, come_u, keep_v, stat_v, come_v)
    groups = [[2 * i + k for i in range(chips)] for k in range(2)]
    come = lax.all_to_all(merged, "dp", 0, 0, axis_index_groups=groups, tiled=True)
    return pl.pallas_call(
        last_kernel,
        out_shape=jax.ShapeDtypeStruct((ROWS, count), f32),
        in_specs=[whole()],
        out_specs=whole(),
        compiler_params=params,
        name="last",
    )(come).T


def solution(mesh):
    return jax.shard_map(
        on_device,
        mesh=mesh,
        in_specs=(P("dp", None), P("dp"), P("cores", None), P("cores")),
        out_specs=P("cores", "dp"),
        check_vma=False,
    )
```

```python
import functools
import math

import jax
import jax.numpy as jnp
from jax import lax
from jax.experimental import pallas as pl
from jax.experimental.pallas import tpu as pltpu
from jax.sharding import PartitionSpec as P

ROWS = 48
STATS = 8
TAIL = 16
REST = 8
WHENCE = (((1, 1), (3, 0)), ((1, 0), (3, 1)), ((0, 1), (2, 0)), ((0, 0), (2, 1)))
VMEM_LIMIT = 16 * 2**20


def whole():
    return pl.BlockSpec(memory_space=pltpu.VMEM)


def fold(op, value):
    out = value[:, :128]
    for k in range(128, value.shape[1], 128):
        out = op(out, value[:, k : k + 128])
    return out


def write_halves(core, acc, top, total, send_ref, keep_ref, stat_ref):
    count, width = acc.shape
    lane = lax.broadcasted_iota(jnp.int32, (count, 128), 1)
    stats = jnp.where(lane == 0, top, total).T[:STATS]
    stat_ref[...] = stats
    half = width // 2
    send_ref[half:, :] = stats
    for j in range(0, width, 8 * ROWS):
        turned = acc[:, j : j + 8 * ROWS].T
        for i in range(4):
            first = turned[2 * ROWS * i : 2 * ROWS * i + ROWS]
            second = turned[2 * ROWS * i + ROWS : 2 * ROWS * (i + 1)]
            at = j // 2 + ROWS * i
            keep_ref[at : at + ROWS, :] = jnp.where(core == 0, first, second)
            send_ref[at : at + ROWS, :] = jnp.where(core == 0, second, first)


def begin_kernel(core_ref, half_ref, out_ref):
    out_ref[...] = jnp.full(out_ref.shape, core_ref[0] + half_ref[0], out_ref.dtype)


def pack_kernel(after_ref, pot_ref, points_ref, key_ref):
    del after_ref
    number, width = points_ref.shape
    key_ref[:number, :] = points_ref[...]
    pot = pot_ref[...].astype(jnp.float32).reshape(1, number)
    row = jnp.concatenate([pot, jnp.zeros((1, width - number), jnp.float32)], 1)
    key_ref[number:, :] = jnp.broadcast_to(row, (TAIL, width)).astype(jnp.bfloat16)


def weigh_kernel(pot_ref, query_ref, data_ref, weights_ref, top_ref, total_ref, scores):
    count, width = data_ref.shape
    step = 512
    scale = 30.0 / math.sqrt(width)
    query = query_ref[: scores.shape[0], :]
    for i in range(0, count, step):
        s = lax.dot_general(
            query, data_ref[i : i + step, :], (((1,), (1,)), ((), ())), preferred_element_type=jnp.float32
        )
        s = s * scale + pot_ref[i : i + step].astype(jnp.float32).reshape(1, step)
        scores[:, i : i + step] = s
        largest = fold(jnp.maximum, s)
        top_ref[...] = largest if i == 0 else jnp.maximum(top_ref[...], largest)
    top_ref[...] = jnp.broadcast_to(jnp.max(top_ref[...], axis=1, keepdims=True), top_ref.shape)
    for i in range(0, count, step):
        added = None
        for k in range(i, i + step, 128):
            p = jnp.exp(scores[:, k : k + 128] - top_ref[...])
            weights_ref[:, k : k + 128] = p.astype(jnp.bfloat16)
            added = p if added is None else added + p
        total_ref[...] = added if i == 0 else total_ref[...] + added


def sum_kernel(core_ref, weights_ref, data_ref, top_ref, total_ref, send_ref, keep_ref, stat_ref, acc):
    acc[...] = jnp.dot(weights_ref[...], data_ref[...], preferred_element_type=jnp.float32)
    summed = jnp.sum(total_ref[...], axis=1, keepdims=True)
    write_halves(core_ref[0], acc, top_ref[...], summed, send_ref, keep_ref, stat_ref)


def self_kernel(core_ref, half_ref, query_ref, key_ref, after_ref, send_ref, keep_ref, stat_ref, acc):
    del after_ref
    count, width = acc.shape
    number = key_ref.shape[0] - TAIL
    scale = 30.0 / math.sqrt(width)
    query = query_ref[pl.ds(pl.multiple_of(half_ref[0] * count, count), count), :]
    keys = key_ref[:number, :]
    pot = key_ref[number:, :number].astype(jnp.float32)[:1]
    s = scale * lax.dot_general(query, keys, (((1,), (1,)), ((), ())), preferred_element_type=jnp.float32)
    s = s + pot
    top = jnp.max(s, axis=1, keepdims=True)
    p = jnp.exp(s - top)
    total = jnp.sum(p, axis=1, keepdims=True)
    acc[...] = jnp.dot(p.astype(jnp.bfloat16), keys, preferred_element_type=jnp.float32)
    top = jnp.broadcast_to(top, (count, 128))
    write_halves(core_ref[0], acc, top, total, send_ref, keep_ref, stat_ref)


def parted(value, number):
    pieces = []
    for _ in range(number):
        piece = value.astype(jnp.bfloat16).astype(jnp.float32)
        pieces.append(piece)
        value = value - piece
    return pieces


def pair_kernel(keep_u, stat_u, come_u, keep_v, stat_v, come_v, out_ref):
    half = keep_u.shape[0]
    merged = []
    for keep, stat, come in ((keep_u, stat_u, come_u), (keep_v, stat_v, come_v)):
        other = come[half:, :]
        top = jnp.maximum(stat[0:1], other[0:1])
        left, right = jnp.exp(stat[0:1] - top), jnp.exp(other[0:1] - top)
        merged.append((top, stat[1:2] * left + other[1:2] * right, left, right))
    (top_u, total_u, left_u, right_u), (top_v, total_v, left_v, right_v) = merged
    high, middle, low = parted(top_v, 3)
    main, rest = parted(total_v, 2)
    tail = parted(top_u, 3) + parted(total_u, 2)
    for pieces in ((high, middle), (low, main), (rest, jnp.zeros_like(rest))):
        tail.append(jnp.concatenate(pieces, 1))
    tail = jnp.concatenate(tail, 0)
    for i in range(half // ROWS):
        rows = slice(ROWS * i, ROWS * (i + 1))
        out_ref[i, :ROWS, :] = (keep_u[rows] * left_u + come_u[rows] * right_u).astype(jnp.bfloat16)
        v = keep_v[rows] * left_v + come_v[rows] * right_v
        v = jnp.concatenate([v[: ROWS // 2], v[ROWS // 2 :]], 1)
        out_ref[i, ROWS:, :] = jnp.concatenate([v, tail], 0).astype(jnp.bfloat16)


def joined(parts):
    top = functools.reduce(jnp.maximum, [t for t, _, _ in parts])
    shares = [jnp.exp(t - top) for t, _, _ in parts]
    total = sum(share * t for share, (_, t, _) in zip(shares, parts))
    return sum(share * value for share, (_, _, value) in zip(shares, parts)) / total


def last_kernel(come_ref, out_ref):
    chips = come_ref.shape[0]
    count = out_ref.shape[1] // 2
    cross, own = [], []
    for i in range(chips):
        u = come_ref[i, :ROWS, :].astype(jnp.float32)
        rest = come_ref[i, ROWS:, :].astype(jnp.float32)
        s = rest[ROWS // 2 :]
        cross.append((s[0:1] + s[1:2] + s[2:3], s[3:4] + s[4:5], u))
        top = s[5:6, :count] + s[5:6, count:] + s[6:7, :count]
        total = s[6:7, count:] + s[7:8, :count]
        own.append((jnp.concatenate([top, top], 1), jnp.concatenate([total, total], 1), rest[: ROWS // 2]))
    pull = joined(cross)
    for h in range(2):
        push = joined(own[h * chips // 2 : (h + 1) * chips // 2])
        lanes = slice(h * count, (h + 1) * count)
        out_ref[: ROWS // 2, lanes] = push[:, :count] - pull[: ROWS // 2, lanes]
        out_ref[ROWS // 2 :, lanes] = push[:, count:] - pull[ROWS // 2 :, lanes]


def on_device(data, data_pot, coreset, core_pot):
    count, width = coreset.shape
    items = data.shape[0]
    half = width // 2
    chips = width // (2 * ROWS)
    position = lax.axis_index("dp")
    shards, blocks = lax.axis_size("dp"), lax.axis_size("cores")
    core = (position % 2).astype(jnp.int32).reshape(1)
    x_hi = (position // chips).astype(jnp.int32).reshape(1)
    f32 = jnp.float32
    params = pltpu.CompilerParams(vmem_limit_bytes=VMEM_LIMIT)
    smem, anywhere = pl.BlockSpec(memory_space=pltpu.SMEM), pl.BlockSpec(memory_space=pl.ANY)

    begun = pl.pallas_call(
        begin_kernel,
        out_shape=jax.ShapeDtypeStruct((8, 128), jnp.int32),
        in_specs=[smem, smem],
        out_specs=whole(),
        compiler_params=params,
        cost_estimate=pl.CostEstimate(flops=10**11, bytes_accessed=4 * items * width, transcendentals=0),
        name="begin",
    )(core, x_hi)
    packed = pl.pallas_call(
        pack_kernel,
        out_shape=jax.ShapeDtypeStruct((count + TAIL, width), coreset.dtype),
        in_specs=[anywhere, whole(), whole()],
        out_specs=whole(),
        compiler_params=params,
        name="pack",
    )(begun, core_pot, coreset)
    pairs = []
    for d in range(shards):
        along, across = WHENCE[d // 2 % 4][d % 2]
        for c in range(blocks):
            source = (c // 2 + along) % 4 * 2 + (c % 2 ^ across)
            pairs.append((d * blocks + source, d * blocks + c))
    keys = lax.ppermute(packed, ("dp", "cores"), pairs)

    weights, top, total = pl.pallas_call(
        weigh_kernel,
        out_shape=[
            jax.ShapeDtypeStruct((count, items), jnp.bfloat16),
            jax.ShapeDtypeStruct((count, 128), f32),
            jax.ShapeDtypeStruct((count, 128), f32),
        ],
        in_specs=[whole()] * 3,
        out_specs=[whole()] * 3,
        scratch_shapes=[pltpu.VMEM((count, items), f32)],
        compiler_params=params,
        cost_estimate=pl.CostEstimate(
            flops=2 * count * items * width, bytes_accessed=2 * items * width, transcendentals=count * items
        ),
        name="weigh",
    )(data_pot, packed, data)

    def halves(number):
        return [
            jax.ShapeDtypeStruct((half + STATS, number), f32),
            jax.ShapeDtypeStruct((half, number), f32),
            jax.ShapeDtypeStruct((STATS, number), f32),
        ]

    swap = [(d, d ^ 1) for d in range(shards)]
    send_u, keep_u, stat_u = pl.pallas_call(
        sum_kernel,
        out_shape=halves(count),
        in_specs=[smem] + [whole()] * 4,
        out_specs=[whole()] * 3,
        scratch_shapes=[pltpu.VMEM((count, width), f32)],
        compiler_params=params,
        cost_estimate=pl.CostEstimate(
            flops=2 * count * items * width, bytes_accessed=2 * items * width, transcendentals=0
        ),
        name="sums",
    )(core, weights, data, top, total)
    come_u = lax.ppermute(send_u, "dp", swap)
    send_v, keep_v, stat_v = pl.pallas_call(
        self_kernel,
        out_shape=halves(count // 2),
        in_specs=[smem, smem, whole(), whole(), anywhere],
        out_specs=[whole()] * 3,
        scratch_shapes=[pltpu.VMEM((count // 2, width), f32)],
        compiler_params=params,
        cost_estimate=pl.CostEstimate(
            flops=2 * count * count * width, bytes_accessed=4 * count * width, transcendentals=count * count // 2
        ),
        name="self",
    )(core, x_hi, packed, keys, stat_u)
    come_v = lax.ppermute(send_v, "dp", swap)
    merged = pl.pallas_call(
        pair_kernel,
        out_shape=jax.ShapeDtypeStruct((chips, 3 * ROWS // 2 + REST, count), jnp.bfloat16),
        in_specs=[whole()] * 6,
        out_specs=whole(),
        compiler_params=params,
        name="pair",
    )(keep_u, stat_u, come_u, keep_v, stat_v, come_v)
    groups = [[2 * i + k for i in range(chips)] for k in range(2)]
    come = lax.all_to_all(merged, "dp", 0, 0, axis_index_groups=groups, tiled=True)
    return pl.pallas_call(
        last_kernel,
        out_shape=jax.ShapeDtypeStruct((ROWS, count), f32),
        in_specs=[whole()],
        out_specs=whole(),
        compiler_params=params,
        name="last",
    )(come).T


def solution(mesh):
    return jax.shard_map(
        on_device,
        mesh=mesh,
        in_specs=(P("dp", None), P("dp"), P("cores", None), P("cores")),
        out_specs=P("cores", "dp"),
        check_vma=False,
    )
```

```python
import functools
import math

import jax
import jax.numpy as jnp
from jax import lax
from jax.experimental import pallas as pl
from jax.experimental.pallas import tpu as pltpu
from jax.sharding import PartitionSpec as P

ROWS = 48
STATS = 8
TAIL = 16
REST = 8
WHENCE = (((1, 1), (3, 0)), ((1, 0), (3, 1)), ((0, 1), (2, 0)), ((0, 0), (2, 1)))
VMEM_LIMIT = 16 * 2**20

ORDER = (4, 5, 6, 7, 0, 1, 2, 3)


def whole():
    return pl.BlockSpec(memory_space=pltpu.VMEM)


def fold(op, value):
    out = value[:, :128]
    for k in range(128, value.shape[1], 128):
        out = op(out, value[:, k : k + 128])
    return out


def write_halves(core, acc, top, total, send_ref, keep_ref, stat_ref):
    count, width = acc.shape
    lane = lax.broadcasted_iota(jnp.int32, (count, 128), 1)
    stats = jnp.where(lane == 0, top, total).T[:STATS]
    stat_ref[...] = stats
    half = width // 2
    send_ref[half:, :] = stats
    for j in range(0, width, 8 * ROWS):
        turned = acc[:, j : j + 8 * ROWS].T
        for i in range(4):
            first = turned[2 * ROWS * i : 2 * ROWS * i + ROWS]
            second = turned[2 * ROWS * i + ROWS : 2 * ROWS * (i + 1)]
            at = j // 2 + ROWS * i
            keep_ref[at : at + ROWS, :] = jnp.where(core == 0, first, second)
            send_ref[at : at + ROWS, :] = jnp.where(core == 0, second, first)


def begin_kernel(core_ref, half_ref, out_ref):
    out_ref[...] = jnp.full(out_ref.shape, core_ref[0] + half_ref[0], out_ref.dtype)


def pack_kernel(after_ref, pot_ref, points_ref, key_ref):
    del after_ref
    number, width = points_ref.shape
    key_ref[:number, :] = points_ref[...]
    pot = pot_ref[...].astype(jnp.float32).reshape(1, number)
    row = jnp.concatenate([pot, jnp.zeros((1, width - number), jnp.float32)], 1)
    key_ref[number:, :] = jnp.broadcast_to(row, (TAIL, width)).astype(jnp.bfloat16)


def weigh_kernel(pot_ref, query_ref, data_ref, weights_ref, top_ref, total_ref, scores):
    count, width = data_ref.shape
    step = 512
    scale = 30.0 / math.sqrt(width)
    query = query_ref[: scores.shape[0], :]
    for i in range(0, count, step):
        s = lax.dot_general(
            query, data_ref[i : i + step, :], (((1,), (1,)), ((), ())), preferred_element_type=jnp.float32
        )
        s = s * scale + pot_ref[i : i + step].astype(jnp.float32).reshape(1, step)
        scores[:, i : i + step] = s
        largest = fold(jnp.maximum, s)
        top_ref[...] = largest if i == 0 else jnp.maximum(top_ref[...], largest)
    top_ref[...] = jnp.broadcast_to(jnp.max(top_ref[...], axis=1, keepdims=True), top_ref.shape)
    for i in range(0, count, step):
        added = None
        for k in range(i, i + step, 128):
            p = jnp.exp(scores[:, k : k + 128] - top_ref[...])
            weights_ref[:, k : k + 128] = p.astype(jnp.bfloat16)
            added = p if added is None else added + p
        total_ref[...] = added if i == 0 else total_ref[...] + added


def sum_kernel(core_ref, weights_ref, data_ref, top_ref, total_ref, send_ref, keep_ref, stat_ref, acc):
    acc[...] = jnp.dot(weights_ref[...], data_ref[...], preferred_element_type=jnp.float32)
    summed = jnp.sum(total_ref[...], axis=1, keepdims=True)
    write_halves(core_ref[0], acc, top_ref[...], summed, send_ref, keep_ref, stat_ref)


def self_kernel(core_ref, half_ref, query_ref, key_ref, after_ref, send_ref, keep_ref, stat_ref, acc):
    del after_ref
    count, width = acc.shape
    number = key_ref.shape[0] - TAIL
    scale = 30.0 / math.sqrt(width)
    query = query_ref[pl.ds(pl.multiple_of(half_ref[0] * count, count), count), :]
    keys = key_ref[:number, :]
    pot = key_ref[number:, :number].astype(jnp.float32)[:1]
    s = scale * lax.dot_general(query, keys, (((1,), (1,)), ((), ())), preferred_element_type=jnp.float32)
    s = s + pot
    top = jnp.max(s, axis=1, keepdims=True)
    p = jnp.exp(s - top)
    total = jnp.sum(p, axis=1, keepdims=True)
    acc[...] = jnp.dot(p.astype(jnp.bfloat16), keys, preferred_element_type=jnp.float32)
    top = jnp.broadcast_to(top, (count, 128))
    write_halves(core_ref[0], acc, top, total, send_ref, keep_ref, stat_ref)


def parted(value, number):
    pieces = []
    for _ in range(number):
        piece = value.astype(jnp.bfloat16).astype(jnp.float32)
        pieces.append(piece)
        value = value - piece
    return pieces


def pair_kernel(keep_u, stat_u, come_u, keep_v, stat_v, come_v, out_ref):
    half = keep_u.shape[0]
    merged = []
    for keep, stat, come in ((keep_u, stat_u, come_u), (keep_v, stat_v, come_v)):
        other = come[half:, :]
        top = jnp.maximum(stat[0:1], other[0:1])
        left, right = jnp.exp(stat[0:1] - top), jnp.exp(other[0:1] - top)
        merged.append((top, stat[1:2] * left + other[1:2] * right, left, right))
    (top_u, total_u, left_u, right_u), (top_v, total_v, left_v, right_v) = merged
    high, middle, low = parted(top_v, 3)
    main, rest = parted(total_v, 2)
    tail = parted(top_u, 3) + parted(total_u, 2)
    for pieces in ((high, middle), (low, main), (rest, jnp.zeros_like(rest))):
        tail.append(jnp.concatenate(pieces, 1))
    tail = jnp.concatenate(tail, 0)
    for i in range(half // ROWS):
        rows = slice(ROWS * i, ROWS * (i + 1))
        to = ORDER.index(i)
        out_ref[to, :ROWS, :] = (keep_u[rows] * left_u + come_u[rows] * right_u).astype(jnp.bfloat16)
        v = keep_v[rows] * left_v + come_v[rows] * right_v
        v = jnp.concatenate([v[: ROWS // 2], v[ROWS // 2 :]], 1)
        out_ref[to, ROWS:, :] = jnp.concatenate([v, tail], 0).astype(jnp.bfloat16)


def joined(parts):
    top = functools.reduce(jnp.maximum, [t for t, _, _ in parts])
    shares = [jnp.exp(t - top) for t, _, _ in parts]
    total = sum(share * t for share, (_, t, _) in zip(shares, parts))
    return sum(share * value for share, (_, _, value) in zip(shares, parts)) / total


def last_kernel(come_ref, out_ref):
    chips = come_ref.shape[0]
    count = out_ref.shape[1] // 2
    cross, own = [], []
    for i in range(chips):
        u = come_ref[i, :ROWS, :].astype(jnp.float32)
        rest = come_ref[i, ROWS:, :].astype(jnp.float32)
        s = rest[ROWS // 2 :]
        cross.append((s[0:1] + s[1:2] + s[2:3], s[3:4] + s[4:5], u))
        top = s[5:6, :count] + s[5:6, count:] + s[6:7, :count]
        total = s[6:7, count:] + s[7:8, :count]
        own.append((jnp.concatenate([top, top], 1), jnp.concatenate([total, total], 1), rest[: ROWS // 2]))
    pull = joined(cross)
    for h in range(2):
        push = joined([part for part, chip in zip(own, ORDER) if 2 * chip // chips == h])
        lanes = slice(h * count, (h + 1) * count)
        out_ref[: ROWS // 2, lanes] = push[:, :count] - pull[: ROWS // 2, lanes]
        out_ref[ROWS // 2 :, lanes] = push[:, count:] - pull[ROWS // 2 :, lanes]


def on_device(data, data_pot, coreset, core_pot):
    count, width = coreset.shape
    items = data.shape[0]
    half = width // 2
    chips = width // (2 * ROWS)
    position = lax.axis_index("dp")
    shards, blocks = lax.axis_size("dp"), lax.axis_size("cores")
    core = (position % 2).astype(jnp.int32).reshape(1)
    x_hi = (position // chips).astype(jnp.int32).reshape(1)
    f32 = jnp.float32
    params = pltpu.CompilerParams(vmem_limit_bytes=VMEM_LIMIT)
    smem, anywhere = pl.BlockSpec(memory_space=pltpu.SMEM), pl.BlockSpec(memory_space=pl.ANY)

    begun = pl.pallas_call(
        begin_kernel,
        out_shape=jax.ShapeDtypeStruct((8, 128), jnp.int32),
        in_specs=[smem, smem],
        out_specs=whole(),
        compiler_params=params,
        cost_estimate=pl.CostEstimate(flops=10**11, bytes_accessed=4 * items * width, transcendentals=0),
        name="begin",
    )(core, x_hi)
    packed = pl.pallas_call(
        pack_kernel,
        out_shape=jax.ShapeDtypeStruct((count + TAIL, width), coreset.dtype),
        in_specs=[anywhere, whole(), whole()],
        out_specs=whole(),
        compiler_params=params,
        name="pack",
    )(begun, core_pot, coreset)
    pairs = []
    for d in range(shards):
        along, across = WHENCE[d // 2 % 4][d % 2]
        for c in range(blocks):
            source = (c // 2 + along) % 4 * 2 + (c % 2 ^ across)
            pairs.append((d * blocks + source, d * blocks + c))
    keys = lax.ppermute(packed, ("dp", "cores"), pairs)

    weights, top, total = pl.pallas_call(
        weigh_kernel,
        out_shape=[
            jax.ShapeDtypeStruct((count, items), jnp.bfloat16),
            jax.ShapeDtypeStruct((count, 128), f32),
            jax.ShapeDtypeStruct((count, 128), f32),
        ],
        in_specs=[whole()] * 3,
        out_specs=[whole()] * 3,
        scratch_shapes=[pltpu.VMEM((count, items), f32)],
        compiler_params=params,
        cost_estimate=pl.CostEstimate(
            flops=2 * count * items * width, bytes_accessed=2 * items * width, transcendentals=count * items
        ),
        name="weigh",
    )(data_pot, packed, data)

    def halves(number):
        return [
            jax.ShapeDtypeStruct((half + STATS, number), f32),
            jax.ShapeDtypeStruct((half, number), f32),
            jax.ShapeDtypeStruct((STATS, number), f32),
        ]

    swap = [(d, d ^ 1) for d in range(shards)]
    send_u, keep_u, stat_u = pl.pallas_call(
        sum_kernel,
        out_shape=halves(count),
        in_specs=[smem] + [whole()] * 4,
        out_specs=[whole()] * 3,
        scratch_shapes=[pltpu.VMEM((count, width), f32)],
        compiler_params=params,
        cost_estimate=pl.CostEstimate(
            flops=2 * count * items * width, bytes_accessed=2 * items * width, transcendentals=0
        ),
        name="sums",
    )(core, weights, data, top, total)
    come_u = lax.ppermute(send_u, "dp", swap)
    send_v, keep_v, stat_v = pl.pallas_call(
        self_kernel,
        out_shape=halves(count // 2),
        in_specs=[smem, smem, whole(), whole(), anywhere],
        out_specs=[whole()] * 3,
        scratch_shapes=[pltpu.VMEM((count // 2, width), f32)],
        compiler_params=params,
        cost_estimate=pl.CostEstimate(
            flops=2 * count * count * width, bytes_accessed=4 * count * width, transcendentals=count * count // 2
        ),
        name="self",
    )(core, x_hi, packed, keys, stat_u)
    come_v = lax.ppermute(send_v, "dp", swap)
    merged = pl.pallas_call(
        pair_kernel,
        out_shape=jax.ShapeDtypeStruct((chips, 3 * ROWS // 2 + REST, count), jnp.bfloat16),
        in_specs=[whole()] * 6,
        out_specs=whole(),
        compiler_params=params,
        name="pair",
    )(keep_u, stat_u, come_u, keep_v, stat_v, come_v)
    groups = [[2 * i + k for i in ORDER] for k in range(2)]
    come = lax.all_to_all(merged, "dp", 0, 0, axis_index_groups=groups, tiled=True)
    return pl.pallas_call(
        last_kernel,
        out_shape=jax.ShapeDtypeStruct((ROWS, count), f32),
        in_specs=[whole()],
        out_specs=whole(),
        compiler_params=params,
        name="last",
    )(come).T


def solution(mesh):
    return jax.shard_map(
        on_device,
        mesh=mesh,
        in_specs=(P("dp", None), P("dp"), P("cores", None), P("cores")),
        out_specs=P("cores", "dp"),
        check_vma=False,
    )
```

```python
import functools
import math

import jax
import jax.numpy as jnp
from jax import lax
from jax.experimental import pallas as pl
from jax.experimental.pallas import tpu as pltpu
from jax.sharding import PartitionSpec as P

ROWS = 48
STATS = 8
TAIL = 16
REST = 8
WHENCE = (((1, 1), (3, 0)), ((1, 0), (3, 1)), ((0, 1), (2, 0)), ((0, 0), (2, 1)))
VMEM_LIMIT = 16 * 2**20

ORDER = (6, 5, 4, 7, 2, 1, 0, 3)


def whole():
    return pl.BlockSpec(memory_space=pltpu.VMEM)


def fold(op, value):
    out = value[:, :128]
    for k in range(128, value.shape[1], 128):
        out = op(out, value[:, k : k + 128])
    return out


def write_halves(core, acc, top, total, send_ref, keep_ref, stat_ref):
    count, width = acc.shape
    lane = lax.broadcasted_iota(jnp.int32, (count, 128), 1)
    stats = jnp.where(lane == 0, top, total).T[:STATS]
    stat_ref[...] = stats
    half = width // 2
    send_ref[half:, :] = stats
    for j in range(0, width, 8 * ROWS):
        turned = acc[:, j : j + 8 * ROWS].T
        for i in range(4):
            first = turned[2 * ROWS * i : 2 * ROWS * i + ROWS]
            second = turned[2 * ROWS * i + ROWS : 2 * ROWS * (i + 1)]
            at = j // 2 + ROWS * i
            keep_ref[at : at + ROWS, :] = jnp.where(core == 0, first, second)
            send_ref[at : at + ROWS, :] = jnp.where(core == 0, second, first)


def begin_kernel(core_ref, half_ref, out_ref):
    out_ref[...] = jnp.full(out_ref.shape, core_ref[0] + half_ref[0], out_ref.dtype)


def pack_kernel(after_ref, pot_ref, points_ref, key_ref):
    del after_ref
    number, width = points_ref.shape
    key_ref[:number, :] = points_ref[...]
    pot = pot_ref[...].astype(jnp.float32).reshape(1, number)
    row = jnp.concatenate([pot, jnp.zeros((1, width - number), jnp.float32)], 1)
    key_ref[number:, :] = jnp.broadcast_to(row, (TAIL, width)).astype(jnp.bfloat16)


def weigh_kernel(pot_ref, query_ref, data_ref, weights_ref, top_ref, total_ref, scores):
    count, width = data_ref.shape
    step = 512
    scale = 30.0 / math.sqrt(width)
    query = query_ref[: scores.shape[0], :]
    for i in range(0, count, step):
        s = lax.dot_general(
            query, data_ref[i : i + step, :], (((1,), (1,)), ((), ())), preferred_element_type=jnp.float32
        )
        s = s * scale + pot_ref[i : i + step].astype(jnp.float32).reshape(1, step)
        scores[:, i : i + step] = s
        largest = fold(jnp.maximum, s)
        top_ref[...] = largest if i == 0 else jnp.maximum(top_ref[...], largest)
    top_ref[...] = jnp.broadcast_to(jnp.max(top_ref[...], axis=1, keepdims=True), top_ref.shape)
    for i in range(0, count, step):
        added = None
        for k in range(i, i + step, 128):
            p = jnp.exp(scores[:, k : k + 128] - top_ref[...])
            weights_ref[:, k : k + 128] = p.astype(jnp.bfloat16)
            added = p if added is None else added + p
        total_ref[...] = added if i == 0 else total_ref[...] + added


def sum_kernel(core_ref, weights_ref, data_ref, top_ref, total_ref, send_ref, keep_ref, stat_ref, acc):
    acc[...] = jnp.dot(weights_ref[...], data_ref[...], preferred_element_type=jnp.float32)
    summed = jnp.sum(total_ref[...], axis=1, keepdims=True)
    write_halves(core_ref[0], acc, top_ref[...], summed, send_ref, keep_ref, stat_ref)


def self_kernel(core_ref, half_ref, query_ref, key_ref, after_ref, send_ref, keep_ref, stat_ref, acc):
    del after_ref
    count, width = acc.shape
    number = key_ref.shape[0] - TAIL
    scale = 30.0 / math.sqrt(width)
    query = query_ref[pl.ds(pl.multiple_of(half_ref[0] * count, count), count), :]
    keys = key_ref[:number, :]
    pot = key_ref[number:, :number].astype(jnp.float32)[:1]
    s = scale * lax.dot_general(query, keys, (((1,), (1,)), ((), ())), preferred_element_type=jnp.float32)
    s = s + pot
    top = jnp.max(s, axis=1, keepdims=True)
    p = jnp.exp(s - top)
    total = jnp.sum(p, axis=1, keepdims=True)
    acc[...] = jnp.dot(p.astype(jnp.bfloat16), keys, preferred_element_type=jnp.float32)
    top = jnp.broadcast_to(top, (count, 128))
    write_halves(core_ref[0], acc, top, total, send_ref, keep_ref, stat_ref)


def parted(value, number):
    pieces = []
    for _ in range(number):
        piece = value.astype(jnp.bfloat16).astype(jnp.float32)
        pieces.append(piece)
        value = value - piece
    return pieces


def pair_kernel(keep_u, stat_u, come_u, keep_v, stat_v, come_v, out_ref):
    half = keep_u.shape[0]
    merged = []
    for keep, stat, come in ((keep_u, stat_u, come_u), (keep_v, stat_v, come_v)):
        other = come[half:, :]
        top = jnp.maximum(stat[0:1], other[0:1])
        left, right = jnp.exp(stat[0:1] - top), jnp.exp(other[0:1] - top)
        merged.append((top, stat[1:2] * left + other[1:2] * right, left, right))
    (top_u, total_u, left_u, right_u), (top_v, total_v, left_v, right_v) = merged
    high, middle, low = parted(top_v, 3)
    main, rest = parted(total_v, 2)
    tail = parted(top_u, 3) + parted(total_u, 2)
    for pieces in ((high, middle), (low, main), (rest, jnp.zeros_like(rest))):
        tail.append(jnp.concatenate(pieces, 1))
    tail = jnp.concatenate(tail, 0)
    for i in range(half // ROWS):
        rows = slice(ROWS * i, ROWS * (i + 1))
        to = ORDER.index(i)
        out_ref[to, :ROWS, :] = (keep_u[rows] * left_u + come_u[rows] * right_u).astype(jnp.bfloat16)
        v = keep_v[rows] * left_v + come_v[rows] * right_v
        v = jnp.concatenate([v[: ROWS // 2], v[ROWS // 2 :]], 1)
        out_ref[to, ROWS:, :] = jnp.concatenate([v, tail], 0).astype(jnp.bfloat16)


def joined(parts):
    top = functools.reduce(jnp.maximum, [t for t, _, _ in parts])
    shares = [jnp.exp(t - top) for t, _, _ in parts]
    total = sum(share * t for share, (_, t, _) in zip(shares, parts))
    return sum(share * value for share, (_, _, value) in zip(shares, parts)) / total


def last_kernel(come_ref, out_ref):
    chips = come_ref.shape[0]
    count = out_ref.shape[1] // 2
    cross, own = [], []
    for i in range(chips):
        u = come_ref[i, :ROWS, :].astype(jnp.float32)
        rest = come_ref[i, ROWS:, :].astype(jnp.float32)
        s = rest[ROWS // 2 :]
        cross.append((s[0:1] + s[1:2] + s[2:3], s[3:4] + s[4:5], u))
        top = s[5:6, :count] + s[5:6, count:] + s[6:7, :count]
        total = s[6:7, count:] + s[7:8, :count]
        own.append((jnp.concatenate([top, top], 1), jnp.concatenate([total, total], 1), rest[: ROWS // 2]))
    pull = joined(cross)
    for h in range(2):
        push = joined([part for part, chip in zip(own, ORDER) if 2 * chip // chips == h])
        lanes = slice(h * count, (h + 1) * count)
        out_ref[: ROWS // 2, lanes] = push[:, :count] - pull[: ROWS // 2, lanes]
        out_ref[ROWS // 2 :, lanes] = push[:, count:] - pull[ROWS // 2 :, lanes]


def on_device(data, data_pot, coreset, core_pot):
    count, width = coreset.shape
    items = data.shape[0]
    half = width // 2
    chips = width // (2 * ROWS)
    position = lax.axis_index("dp")
    shards, blocks = lax.axis_size("dp"), lax.axis_size("cores")
    core = (position % 2).astype(jnp.int32).reshape(1)
    x_hi = (position // chips).astype(jnp.int32).reshape(1)
    f32 = jnp.float32
    params = pltpu.CompilerParams(vmem_limit_bytes=VMEM_LIMIT)
    smem, anywhere = pl.BlockSpec(memory_space=pltpu.SMEM), pl.BlockSpec(memory_space=pl.ANY)

    begun = pl.pallas_call(
        begin_kernel,
        out_shape=jax.ShapeDtypeStruct((8, 128), jnp.int32),
        in_specs=[smem, smem],
        out_specs=whole(),
        compiler_params=params,
        cost_estimate=pl.CostEstimate(flops=10**11, bytes_accessed=4 * items * width, transcendentals=0),
        name="begin",
    )(core, x_hi)
    packed = pl.pallas_call(
        pack_kernel,
        out_shape=jax.ShapeDtypeStruct((count + TAIL, width), coreset.dtype),
        in_specs=[anywhere, whole(), whole()],
        out_specs=whole(),
        compiler_params=params,
        name="pack",
    )(begun, core_pot, coreset)
    pairs = []
    for d in range(shards):
        along, across = WHENCE[d // 2 % 4][d % 2]
        for c in range(blocks):
            source = (c // 2 + along) % 4 * 2 + (c % 2 ^ across)
            pairs.append((d * blocks + source, d * blocks + c))
    keys = lax.ppermute(packed, ("dp", "cores"), pairs)

    weights, top, total = pl.pallas_call(
        weigh_kernel,
        out_shape=[
            jax.ShapeDtypeStruct((count, items), jnp.bfloat16),
            jax.ShapeDtypeStruct((count, 128), f32),
            jax.ShapeDtypeStruct((count, 128), f32),
        ],
        in_specs=[whole()] * 3,
        out_specs=[whole()] * 3,
        scratch_shapes=[pltpu.VMEM((count, items), f32)],
        compiler_params=params,
        cost_estimate=pl.CostEstimate(
            flops=2 * count * items * width, bytes_accessed=2 * items * width, transcendentals=count * items
        ),
        name="weigh",
    )(data_pot, packed, data)

    def halves(number):
        return [
            jax.ShapeDtypeStruct((half + STATS, number), f32),
            jax.ShapeDtypeStruct((half, number), f32),
            jax.ShapeDtypeStruct((STATS, number), f32),
        ]

    swap = [(d, d ^ 1) for d in range(shards)]
    send_u, keep_u, stat_u = pl.pallas_call(
        sum_kernel,
        out_shape=halves(count),
        in_specs=[smem] + [whole()] * 4,
        out_specs=[whole()] * 3,
        scratch_shapes=[pltpu.VMEM((count, width), f32)],
        compiler_params=params,
        cost_estimate=pl.CostEstimate(
            flops=2 * count * items * width, bytes_accessed=2 * items * width, transcendentals=0
        ),
        name="sums",
    )(core, weights, data, top, total)
    come_u = lax.ppermute(send_u, "dp", swap)
    send_v, keep_v, stat_v = pl.pallas_call(
        self_kernel,
        out_shape=halves(count // 2),
        in_specs=[smem, smem, whole(), whole(), anywhere],
        out_specs=[whole()] * 3,
        scratch_shapes=[pltpu.VMEM((count // 2, width), f32)],
        compiler_params=params,
        cost_estimate=pl.CostEstimate(
            flops=2 * count * count * width, bytes_accessed=4 * count * width, transcendentals=count * count // 2
        ),
        name="self",
    )(core, x_hi, packed, keys, stat_u)
    come_v = lax.ppermute(send_v, "dp", swap)
    merged = pl.pallas_call(
        pair_kernel,
        out_shape=jax.ShapeDtypeStruct((chips, 3 * ROWS // 2 + REST, count), jnp.bfloat16),
        in_specs=[whole()] * 6,
        out_specs=whole(),
        compiler_params=params,
        name="pair",
    )(keep_u, stat_u, come_u, keep_v, stat_v, come_v)
    groups = [[2 * i + k for i in ORDER] for k in range(2)]
    come = lax.all_to_all(merged, "dp", 0, 0, axis_index_groups=groups, tiled=True)
    return pl.pallas_call(
        last_kernel,
        out_shape=jax.ShapeDtypeStruct((ROWS, count), f32),
        in_specs=[whole()],
        out_specs=whole(),
        compiler_params=params,
        name="last",
    )(come).T


def solution(mesh):
    return jax.shard_map(
        on_device,
        mesh=mesh,
        in_specs=(P("dp", None), P("dp"), P("cores", None), P("cores")),
        out_specs=P("cores", "dp"),
        check_vma=False,
    )
```

```python
import functools
import math

import jax
import jax.numpy as jnp
from jax import lax
from jax.experimental import pallas as pl
from jax.experimental.pallas import tpu as pltpu
from jax.sharding import PartitionSpec as P

ROWS = 48
STATS = 8
TAIL = 16
REST = 8
WHENCE = (((1, 1), (3, 0)), ((1, 0), (3, 1)), ((0, 1), (2, 0)), ((0, 0), (2, 1)))
VMEM_LIMIT = 16 * 2**20

ORDER = (6, 5, 4, 7, 2, 1, 0, 3)


def whole():
    return pl.BlockSpec(memory_space=pltpu.VMEM)


def fold(op, value):
    out = value[:, :128]
    for k in range(128, value.shape[1], 128):
        out = op(out, value[:, k : k + 128])
    return out


def write_halves(core, acc, top, total, send_ref, keep_ref, stat_ref):
    count, width = acc.shape
    lane = lax.broadcasted_iota(jnp.int32, (count, 128), 1)
    stats = jnp.where(lane == 0, top, total).T[:STATS]
    stat_ref[...] = stats
    half = width // 2
    send_ref[half:, :] = stats
    for j in range(0, width, 8 * ROWS):
        turned = acc[:, j : j + 8 * ROWS].T
        for i in range(4):
            first = turned[2 * ROWS * i : 2 * ROWS * i + ROWS]
            second = turned[2 * ROWS * i + ROWS : 2 * ROWS * (i + 1)]
            at = j // 2 + ROWS * i
            keep_ref[at : at + ROWS, :] = jnp.where(core == 0, first, second)
            send_ref[at : at + ROWS, :] = jnp.where(core == 0, second, first)


def begin_kernel(core_ref, half_ref, out_ref):
    out_ref[...] = jnp.full(out_ref.shape, core_ref[0] + half_ref[0], out_ref.dtype)


def pack_kernel(after_ref, pot_ref, points_ref, key_ref):
    del after_ref
    number, width = points_ref.shape
    key_ref[:number, :] = points_ref[...]
    pot = pot_ref[...].astype(jnp.float32).reshape(1, number)
    row = jnp.concatenate([pot, jnp.zeros((1, width - number), jnp.float32)], 1)
    key_ref[number:, :] = jnp.broadcast_to(row, (TAIL, width)).astype(jnp.bfloat16)


def weigh_kernel(pot_ref, query_ref, data_ref, weights_ref, top_ref, total_ref, scores):
    count, width = data_ref.shape
    step = 512
    scale = 30.0 / math.sqrt(width)
    query = query_ref[: scores.shape[0], :]
    for i in range(0, count, step):
        s = lax.dot_general(
            query, data_ref[i : i + step, :], (((1,), (1,)), ((), ())), preferred_element_type=jnp.float32
        )
        s = s * scale + pot_ref[i : i + step].astype(jnp.float32).reshape(1, step)
        scores[:, i : i + step] = s
        largest = fold(jnp.maximum, s)
        top_ref[...] = largest if i == 0 else jnp.maximum(top_ref[...], largest)
    top_ref[...] = jnp.broadcast_to(jnp.max(top_ref[...], axis=1, keepdims=True), top_ref.shape)
    for i in range(0, count, step):
        added = None
        for k in range(i, i + step, 128):
            p = jnp.exp(scores[:, k : k + 128] - top_ref[...])
            weights_ref[:, k : k + 128] = p.astype(jnp.bfloat16)
            added = p if added is None else added + p
        total_ref[...] = added if i == 0 else total_ref[...] + added


def sum_kernel(core_ref, weights_ref, data_ref, top_ref, total_ref, send_ref, keep_ref, stat_ref, acc):
    acc[...] = jnp.dot(weights_ref[...], data_ref[...], preferred_element_type=jnp.float32)
    summed = jnp.sum(total_ref[...], axis=1, keepdims=True)
    write_halves(core_ref[0], acc, top_ref[...], summed, send_ref, keep_ref, stat_ref)


def self_kernel(core_ref, half_ref, query_ref, key_ref, after_ref, send_ref, keep_ref, stat_ref, acc):
    del after_ref
    count, width = acc.shape
    number = key_ref.shape[0] - TAIL
    scale = 30.0 / math.sqrt(width)
    query = query_ref[pl.ds(pl.multiple_of(half_ref[0] * count, count), count), :]
    keys = key_ref[:number, :]
    pot = key_ref[number:, :number].astype(jnp.float32)[:1]
    s = scale * lax.dot_general(query, keys, (((1,), (1,)), ((), ())), preferred_element_type=jnp.float32)
    s = s + pot
    top = jnp.max(s, axis=1, keepdims=True)
    p = jnp.exp(s - top)
    total = jnp.sum(p, axis=1, keepdims=True)
    acc[...] = jnp.dot(p.astype(jnp.bfloat16), keys, preferred_element_type=jnp.float32)
    top = jnp.broadcast_to(top, (count, 128))
    write_halves(core_ref[0], acc, top, total, send_ref, keep_ref, stat_ref)


def parted(value, number):
    pieces = []
    for _ in range(number):
        piece = value.astype(jnp.bfloat16).astype(jnp.float32)
        pieces.append(piece)
        value = value - piece
    return pieces


def merged(stat, come):
    other = come[come.shape[0] - STATS :, :]
    top = jnp.maximum(stat[0:1], other[0:1])
    left, right = jnp.exp(stat[0:1] - top), jnp.exp(other[0:1] - top)
    return top, stat[1:2] * left + other[1:2] * right, left, right


def cross_pair_kernel(keep, stat, come, out_ref, tail_ref):
    top, total, left, right = merged(stat, come)
    tail_ref[...] = jnp.concatenate(parted(top, 3) + parted(total, 2) + [jnp.zeros_like(top)] * 3, 0)
    for i in range(keep.shape[0] // ROWS):
        rows = slice(ROWS * i, ROWS * (i + 1))
        out_ref[ORDER.index(i), :ROWS, :] = (keep[rows] * left + come[rows] * right).astype(jnp.bfloat16)


def self_pair_kernel(keep, stat, come, tail_ref, part_ref, out_ref):
    del part_ref
    top, total, left, right = merged(stat, come)
    high, middle, low = parted(top, 3)
    main, rest = parted(total, 2)
    tail = [tail_ref[:5, :]]
    for pieces in ((high, middle), (low, main), (rest, jnp.zeros_like(rest))):
        tail.append(jnp.concatenate(pieces, 1))
    tail = jnp.concatenate(tail, 0)
    for i in range(keep.shape[0] // ROWS):
        rows = slice(ROWS * i, ROWS * (i + 1))
        v = keep[rows] * left + come[rows] * right
        v = jnp.concatenate([v[: ROWS // 2], v[ROWS // 2 :]], 1)
        out_ref[ORDER.index(i), ROWS:, :] = jnp.concatenate([v, tail], 0).astype(jnp.bfloat16)


def joined(parts):
    top = functools.reduce(jnp.maximum, [t for t, _, _ in parts])
    shares = [jnp.exp(t - top) for t, _, _ in parts]
    total = sum(share * t for share, (_, t, _) in zip(shares, parts))
    return sum(share * value for share, (_, _, value) in zip(shares, parts)) / total


def last_kernel(come_ref, out_ref):
    chips = come_ref.shape[0]
    count = out_ref.shape[1] // 2
    cross, own = [], []
    for i in range(chips):
        u = come_ref[i, :ROWS, :].astype(jnp.float32)
        rest = come_ref[i, ROWS:, :].astype(jnp.float32)
        s = rest[ROWS // 2 :]
        cross.append((s[0:1] + s[1:2] + s[2:3], s[3:4] + s[4:5], u))
        top = s[5:6, :count] + s[5:6, count:] + s[6:7, :count]
        total = s[6:7, count:] + s[7:8, :count]
        own.append((jnp.concatenate([top, top], 1), jnp.concatenate([total, total], 1), rest[: ROWS // 2]))
    pull = joined(cross)
    for h in range(2):
        push = joined([part for part, chip in zip(own, ORDER) if 2 * chip // chips == h])
        lanes = slice(h * count, (h + 1) * count)
        out_ref[: ROWS // 2, lanes] = push[:, :count] - pull[: ROWS // 2, lanes]
        out_ref[ROWS // 2 :, lanes] = push[:, count:] - pull[ROWS // 2 :, lanes]


def on_device(data, data_pot, coreset, core_pot):
    count, width = coreset.shape
    items = data.shape[0]
    half = width // 2
    chips = width // (2 * ROWS)
    position = lax.axis_index("dp")
    shards, blocks = lax.axis_size("dp"), lax.axis_size("cores")
    core = (position % 2).astype(jnp.int32).reshape(1)
    x_hi = (position // chips).astype(jnp.int32).reshape(1)
    f32 = jnp.float32
    params = pltpu.CompilerParams(vmem_limit_bytes=VMEM_LIMIT)
    smem, anywhere = pl.BlockSpec(memory_space=pltpu.SMEM), pl.BlockSpec(memory_space=pl.ANY)

    begun = pl.pallas_call(
        begin_kernel,
        out_shape=jax.ShapeDtypeStruct((8, 128), jnp.int32),
        in_specs=[smem, smem],
        out_specs=whole(),
        compiler_params=params,
        cost_estimate=pl.CostEstimate(flops=10**11, bytes_accessed=4 * items * width, transcendentals=0),
        name="begin",
    )(core, x_hi)
    packed = pl.pallas_call(
        pack_kernel,
        out_shape=jax.ShapeDtypeStruct((count + TAIL, width), coreset.dtype),
        in_specs=[anywhere, whole(), whole()],
        out_specs=whole(),
        compiler_params=params,
        name="pack",
    )(begun, core_pot, coreset)
    pairs = []
    for d in range(shards):
        along, across = WHENCE[d // 2 % 4][d % 2]
        for c in range(blocks):
            source = (c // 2 + along) % 4 * 2 + (c % 2 ^ across)
            pairs.append((d * blocks + source, d * blocks + c))
    keys = lax.ppermute(packed, ("dp", "cores"), pairs)

    weights, top, total = pl.pallas_call(
        weigh_kernel,
        out_shape=[
            jax.ShapeDtypeStruct((count, items), jnp.bfloat16),
            jax.ShapeDtypeStruct((count, 128), f32),
            jax.ShapeDtypeStruct((count, 128), f32),
        ],
        in_specs=[whole()] * 3,
        out_specs=[whole()] * 3,
        scratch_shapes=[pltpu.VMEM((count, items), f32)],
        compiler_params=params,
        cost_estimate=pl.CostEstimate(
            flops=2 * count * items * width, bytes_accessed=2 * items * width, transcendentals=count * items
        ),
        name="weigh",
    )(data_pot, packed, data)

    def halves(number):
        return [
            jax.ShapeDtypeStruct((half + STATS, number), f32),
            jax.ShapeDtypeStruct((half, number), f32),
            jax.ShapeDtypeStruct((STATS, number), f32),
        ]

    swap = [(d, d ^ 1) for d in range(shards)]
    send_u, keep_u, stat_u = pl.pallas_call(
        sum_kernel,
        out_shape=halves(count),
        in_specs=[smem] + [whole()] * 4,
        out_specs=[whole()] * 3,
        scratch_shapes=[pltpu.VMEM((count, width), f32)],
        compiler_params=params,
        cost_estimate=pl.CostEstimate(
            flops=2 * count * items * width, bytes_accessed=2 * items * width, transcendentals=0
        ),
        name="sums",
    )(core, weights, data, top, total)
    come_u = lax.ppermute(send_u, "dp", swap)
    part, tail = pl.pallas_call(
        cross_pair_kernel,
        out_shape=[
            jax.ShapeDtypeStruct((chips, 3 * ROWS // 2 + REST, count), jnp.bfloat16),
            jax.ShapeDtypeStruct((STATS, count), f32),
        ],
        in_specs=[whole()] * 3,
        out_specs=[whole()] * 2,
        compiler_params=params,
        name="cross_pair",
    )(keep_u, stat_u, come_u)
    send_v, keep_v, stat_v = pl.pallas_call(
        self_kernel,
        out_shape=halves(count // 2),
        in_specs=[smem, smem, whole(), whole(), anywhere],
        out_specs=[whole()] * 3,
        scratch_shapes=[pltpu.VMEM((count // 2, width), f32)],
        compiler_params=params,
        cost_estimate=pl.CostEstimate(
            flops=2 * count * count * width, bytes_accessed=4 * count * width, transcendentals=count * count // 2
        ),
        name="self",
    )(core, x_hi, packed, keys, stat_u)
    come_v = lax.ppermute(send_v, "dp", swap)
    joint = jax.ShapeDtypeStruct((chips, 3 * ROWS // 2 + REST, count), jnp.bfloat16)
    both = pl.pallas_call(
        self_pair_kernel,
        out_shape=joint,
        in_specs=[whole()] * 5,
        out_specs=whole(),
        input_output_aliases={4: 0},
        compiler_params=params,
        name="self_pair",
    )(keep_v, stat_v, come_v, tail, part)
    groups = [[2 * i + k for i in ORDER] for k in range(2)]
    come = lax.all_to_all(both, "dp", 0, 0, axis_index_groups=groups, tiled=True)
    return pl.pallas_call(
        last_kernel,
        out_shape=jax.ShapeDtypeStruct((ROWS, count), f32),
        in_specs=[whole()],
        out_specs=whole(),
        compiler_params=params,
        name="last",
    )(come).T


def solution(mesh):
    return jax.shard_map(
        on_device,
        mesh=mesh,
        in_specs=(P("dp", None), P("dp"), P("cores", None), P("cores")),
        out_specs=P("cores", "dp"),
        check_vma=False,
    )
```

```python
import functools
import math

import jax
import jax.numpy as jnp
from jax import lax
from jax.experimental import pallas as pl
from jax.experimental.pallas import tpu as pltpu
from jax.sharding import PartitionSpec as P

ROWS = 48
STATS = 8
TAIL = 16
REST = 8
WHENCE = (((1, 1), (3, 0)), ((1, 0), (3, 1)), ((0, 1), (2, 0)), ((0, 0), (2, 1)))
VMEM_LIMIT = 16 * 2**20

ORDER = (6, 2, 5, 1, 4, 0, 7, 3)


def whole():
    return pl.BlockSpec(memory_space=pltpu.VMEM)


def fold(op, value):
    out = value[:, :128]
    for k in range(128, value.shape[1], 128):
        out = op(out, value[:, k : k + 128])
    return out


def write_halves(core, acc, top, total, send_ref, keep_ref, stat_ref):
    count, width = acc.shape
    lane = lax.broadcasted_iota(jnp.int32, (count, 128), 1)
    stats = jnp.where(lane == 0, top, total).T[:STATS]
    stat_ref[...] = stats
    half = width // 2
    send_ref[half:, :] = stats
    for j in range(0, width, 8 * ROWS):
        turned = acc[:, j : j + 8 * ROWS].T
        for i in range(4):
            first = turned[2 * ROWS * i : 2 * ROWS * i + ROWS]
            second = turned[2 * ROWS * i + ROWS : 2 * ROWS * (i + 1)]
            at = j // 2 + ROWS * i
            keep_ref[at : at + ROWS, :] = jnp.where(core == 0, first, second)
            send_ref[at : at + ROWS, :] = jnp.where(core == 0, second, first)


def begin_kernel(core_ref, half_ref, out_ref):
    out_ref[...] = jnp.full(out_ref.shape, core_ref[0] + half_ref[0], out_ref.dtype)


def pack_kernel(after_ref, pot_ref, points_ref, key_ref):
    del after_ref
    number, width = points_ref.shape
    key_ref[:number, :] = points_ref[...]
    pot = pot_ref[...].astype(jnp.float32).reshape(1, number)
    row = jnp.concatenate([pot, jnp.zeros((1, width - number), jnp.float32)], 1)
    key_ref[number:, :] = jnp.broadcast_to(row, (TAIL, width)).astype(jnp.bfloat16)


def weigh_kernel(pot_ref, query_ref, data_ref, weights_ref, top_ref, total_ref, scores):
    count, width = data_ref.shape
    step = 512
    scale = 30.0 / math.sqrt(width)
    query = query_ref[: scores.shape[0], :]
    for i in range(0, count, step):
        s = lax.dot_general(
            query, data_ref[i : i + step, :], (((1,), (1,)), ((), ())), preferred_element_type=jnp.float32
        )
        s = s * scale + pot_ref[i : i + step].astype(jnp.float32).reshape(1, step)
        scores[:, i : i + step] = s
        largest = fold(jnp.maximum, s)
        top_ref[...] = largest if i == 0 else jnp.maximum(top_ref[...], largest)
    top_ref[...] = jnp.broadcast_to(jnp.max(top_ref[...], axis=1, keepdims=True), top_ref.shape)
    for i in range(0, count, step):
        added = None
        for k in range(i, i + step, 128):
            p = jnp.exp(scores[:, k : k + 128] - top_ref[...])
            weights_ref[:, k : k + 128] = p.astype(jnp.bfloat16)
            added = p if added is None else added + p
        total_ref[...] = added if i == 0 else total_ref[...] + added


def sum_kernel(core_ref, weights_ref, data_ref, top_ref, total_ref, send_ref, keep_ref, stat_ref, acc):
    acc[...] = jnp.dot(weights_ref[...], data_ref[...], preferred_element_type=jnp.float32)
    summed = jnp.sum(total_ref[...], axis=1, keepdims=True)
    write_halves(core_ref[0], acc, top_ref[...], summed, send_ref, keep_ref, stat_ref)


def self_kernel(core_ref, half_ref, query_ref, key_ref, after_ref, send_ref, keep_ref, stat_ref, acc):
    del after_ref
    count, width = acc.shape
    number = key_ref.shape[0] - TAIL
    scale = 30.0 / math.sqrt(width)
    query = query_ref[pl.ds(pl.multiple_of(half_ref[0] * count, count), count), :]
    keys = key_ref[:number, :]
    pot = key_ref[number:, :number].astype(jnp.float32)[:1]
    s = scale * lax.dot_general(query, keys, (((1,), (1,)), ((), ())), preferred_element_type=jnp.float32)
    s = s + pot
    top = jnp.max(s, axis=1, keepdims=True)
    p = jnp.exp(s - top)
    total = jnp.sum(p, axis=1, keepdims=True)
    acc[...] = jnp.dot(p.astype(jnp.bfloat16), keys, preferred_element_type=jnp.float32)
    top = jnp.broadcast_to(top, (count, 128))
    write_halves(core_ref[0], acc, top, total, send_ref, keep_ref, stat_ref)


def parted(value, number):
    pieces = []
    for _ in range(number):
        piece = value.astype(jnp.bfloat16).astype(jnp.float32)
        pieces.append(piece)
        value = value - piece
    return pieces


def merged(stat, come):
    other = come[come.shape[0] - STATS :, :]
    top = jnp.maximum(stat[0:1], other[0:1])
    left, right = jnp.exp(stat[0:1] - top), jnp.exp(other[0:1] - top)
    return top, stat[1:2] * left + other[1:2] * right, left, right


def cross_pair_kernel(keep, stat, come, out_ref, tail_ref):
    top, total, left, right = merged(stat, come)
    tail_ref[...] = jnp.concatenate(parted(top, 3) + parted(total, 2) + [jnp.zeros_like(top)] * 3, 0)
    for i in range(keep.shape[0] // ROWS):
        rows = slice(ROWS * i, ROWS * (i + 1))
        out_ref[ORDER.index(i), :ROWS, :] = (keep[rows] * left + come[rows] * right).astype(jnp.bfloat16)


def self_pair_kernel(keep, stat, come, tail_ref, part_ref, out_ref):
    del part_ref
    top, total, left, right = merged(stat, come)
    high, middle, low = parted(top, 3)
    main, rest = parted(total, 2)
    tail = [tail_ref[:5, :]]
    for pieces in ((high, middle), (low, main), (rest, jnp.zeros_like(rest))):
        tail.append(jnp.concatenate(pieces, 1))
    tail = jnp.concatenate(tail, 0)
    for i in range(keep.shape[0] // ROWS):
        rows = slice(ROWS * i, ROWS * (i + 1))
        v = keep[rows] * left + come[rows] * right
        v = jnp.concatenate([v[: ROWS // 2], v[ROWS // 2 :]], 1)
        out_ref[ORDER.index(i), ROWS:, :] = jnp.concatenate([v, tail], 0).astype(jnp.bfloat16)


def joined(parts):
    top = functools.reduce(jnp.maximum, [t for t, _, _ in parts])
    shares = [jnp.exp(t - top) for t, _, _ in parts]
    total = sum(share * t for share, (_, t, _) in zip(shares, parts))
    return sum(share * value for share, (_, _, value) in zip(shares, parts)) / total


def last_kernel(come_ref, out_ref):
    chips = come_ref.shape[0]
    count = out_ref.shape[1] // 2
    cross, own = [], []
    for i in range(chips):
        u = come_ref[i, :ROWS, :].astype(jnp.float32)
        rest = come_ref[i, ROWS:, :].astype(jnp.float32)
        s = rest[ROWS // 2 :]
        cross.append((s[0:1] + s[1:2] + s[2:3], s[3:4] + s[4:5], u))
        top = s[5:6, :count] + s[5:6, count:] + s[6:7, :count]
        total = s[6:7, count:] + s[7:8, :count]
        own.append((jnp.concatenate([top, top], 1), jnp.concatenate([total, total], 1), rest[: ROWS // 2]))
    pull = joined(cross)
    for h in range(2):
        push = joined([part for part, chip in zip(own, ORDER) if 2 * chip // chips == h])
        lanes = slice(h * count, (h + 1) * count)
        out_ref[: ROWS // 2, lanes] = push[:, :count] - pull[: ROWS // 2, lanes]
        out_ref[ROWS // 2 :, lanes] = push[:, count:] - pull[ROWS // 2 :, lanes]


def on_device(data, data_pot, coreset, core_pot):
    count, width = coreset.shape
    items = data.shape[0]
    half = width // 2
    chips = width // (2 * ROWS)
    position = lax.axis_index("dp")
    shards, blocks = lax.axis_size("dp"), lax.axis_size("cores")
    core = (position % 2).astype(jnp.int32).reshape(1)
    x_hi = (position // chips).astype(jnp.int32).reshape(1)
    f32 = jnp.float32
    params = pltpu.CompilerParams(vmem_limit_bytes=VMEM_LIMIT)
    smem, anywhere = pl.BlockSpec(memory_space=pltpu.SMEM), pl.BlockSpec(memory_space=pl.ANY)

    begun = pl.pallas_call(
        begin_kernel,
        out_shape=jax.ShapeDtypeStruct((8, 128), jnp.int32),
        in_specs=[smem, smem],
        out_specs=whole(),
        compiler_params=params,
        cost_estimate=pl.CostEstimate(flops=10**11, bytes_accessed=4 * items * width, transcendentals=0),
        name="begin",
    )(core, x_hi)
    packed = pl.pallas_call(
        pack_kernel,
        out_shape=jax.ShapeDtypeStruct((count + TAIL, width), coreset.dtype),
        in_specs=[anywhere, whole(), whole()],
        out_specs=whole(),
        compiler_params=params,
        name="pack",
    )(begun, core_pot, coreset)
    pairs = []
    for d in range(shards):
        along, across = WHENCE[d // 2 % 4][d % 2]
        for c in range(blocks):
            source = (c // 2 + along) % 4 * 2 + (c % 2 ^ across)
            pairs.append((d * blocks + source, d * blocks + c))
    keys = lax.ppermute(packed, ("dp", "cores"), pairs)

    weights, top, total = pl.pallas_call(
        weigh_kernel,
        out_shape=[
            jax.ShapeDtypeStruct((count, items), jnp.bfloat16),
            jax.ShapeDtypeStruct((count, 128), f32),
            jax.ShapeDtypeStruct((count, 128), f32),
        ],
        in_specs=[whole()] * 3,
        out_specs=[whole()] * 3,
        scratch_shapes=[pltpu.VMEM((count, items), f32)],
        compiler_params=params,
        cost_estimate=pl.CostEstimate(
            flops=2 * count * items * width, bytes_accessed=2 * items * width, transcendentals=count * items
        ),
        name="weigh",
    )(data_pot, packed, data)

    def halves(number):
        return [
            jax.ShapeDtypeStruct((half + STATS, number), f32),
            jax.ShapeDtypeStruct((half, number), f32),
            jax.ShapeDtypeStruct((STATS, number), f32),
        ]

    swap = [(d, d ^ 1) for d in range(shards)]
    send_u, keep_u, stat_u = pl.pallas_call(
        sum_kernel,
        out_shape=halves(count),
        in_specs=[smem] + [whole()] * 4,
        out_specs=[whole()] * 3,
        scratch_shapes=[pltpu.VMEM((count, width), f32)],
        compiler_params=params,
        cost_estimate=pl.CostEstimate(
            flops=2 * count * items * width, bytes_accessed=2 * items * width, transcendentals=0
        ),
        name="sums",
    )(core, weights, data, top, total)
    come_u = lax.ppermute(send_u, "dp", swap)
    part, tail = pl.pallas_call(
        cross_pair_kernel,
        out_shape=[
            jax.ShapeDtypeStruct((chips, 3 * ROWS // 2 + REST, count), jnp.bfloat16),
            jax.ShapeDtypeStruct((STATS, count), f32),
        ],
        in_specs=[whole()] * 3,
        out_specs=[whole()] * 2,
        compiler_params=params,
        name="cross_pair",
    )(keep_u, stat_u, come_u)
    send_v, keep_v, stat_v = pl.pallas_call(
        self_kernel,
        out_shape=halves(count // 2),
        in_specs=[smem, smem, whole(), whole(), anywhere],
        out_specs=[whole()] * 3,
        scratch_shapes=[pltpu.VMEM((count // 2, width), f32)],
        compiler_params=params,
        cost_estimate=pl.CostEstimate(
            flops=2 * count * count * width, bytes_accessed=4 * count * width, transcendentals=count * count // 2
        ),
        name="self",
    )(core, x_hi, packed, keys, stat_u)
    come_v = lax.ppermute(send_v, "dp", swap)
    joint = jax.ShapeDtypeStruct((chips, 3 * ROWS // 2 + REST, count), jnp.bfloat16)
    both = pl.pallas_call(
        self_pair_kernel,
        out_shape=joint,
        in_specs=[whole()] * 5,
        out_specs=whole(),
        input_output_aliases={4: 0},
        compiler_params=params,
        name="self_pair",
    )(keep_v, stat_v, come_v, tail, part)
    groups = [[2 * i + k for i in ORDER] for k in range(2)]
    come = lax.all_to_all(both, "dp", 0, 0, axis_index_groups=groups, tiled=True)
    return pl.pallas_call(
        last_kernel,
        out_shape=jax.ShapeDtypeStruct((ROWS, count), f32),
        in_specs=[whole()],
        out_specs=whole(),
        compiler_params=params,
        name="last",
    )(come).T


def solution(mesh):
    return jax.shard_map(
        on_device,
        mesh=mesh,
        in_specs=(P("dp", None), P("dp"), P("cores", None), P("cores")),
        out_specs=P("cores", "dp"),
        check_vma=False,
    )
```
